32 devices in a mesh: dp: 4 (over y, x), shard: 8 (over z, core).
Axes of the slice: x: 2, y: 2, z: 4, core: 2. Of those that a mesh axis runs over, the one named last changes fastest.
Arguments:
- hot_ids: int32 [4096, 8], P(('dp', 'shard')), may hold values from 0 to 4095
- cold_owner: int32 [8192, 1], P(('dp', 'shard')), may hold values from 0 to 7; in each aligned block of 256 rows (0 to 255, 256 to 511, ...) at most 64 rows name the same one
- cold_offset: int32 [8192], P(('dp', 'shard')), may hold values from 0 to 4095
- hot_table: bfloat16 [4096, 128], replicated, may hold values from -2 to 2
- cold_table: bfloat16 [32768, 128], P('shard'), may hold values from -4 to 4
- w_in: bfloat16 [256, 4096], P(None, 'shard'), may hold values from -0.375 to 0.375
- bias_in: bfloat16 [1, 4096], P(None, 'shard'), may hold values from -0.59765625 to 0.59765625
- w_out: bfloat16 [1, 4096], P(None, 'shard'), may hold values from -0.1875 to 0.1875
- cotangent: float32 [4096], P(('dp', 'shard')), may hold values from -10 to 10
Outputs:
- logits: float32 [4096], P(('dp', 'shard'))
- hot_grad: bfloat16 [4096, 128], P('shard')
- cold_grad: bfloat16 [32768, 128], P('shard')
- w_in_grad: float32 [256, 4096], P(None, 'shard')
The draws below stay inside these ranges and needn't reach their ends.
Inputs may be any that keep to these rules, and one draw needn't show every extreme that they name: `cold_owner`: within the 256 cold lookups of one device no owner is named more than 64 times, a bound that some block reaches.
All inputs are finite; a program needn't handle non-finite values.
Results may differ from the reference program's by a relative error of at most 0.015.
Values may be sent and summed in bfloat16 or wider, within the bound.
A program may use at most 64 MiB of HBM per device.

```python
import math
import jax
import jax.numpy as jnp
import numpy as np
from jax import lax

E = 128
H = 4096
HOT = 4096
COLD_DEV = 4096
L_HOT = 8
L_COLD = 2
B_DEV = 128
D_IN = 256
SAMPLES = 4096
COLD = 32768
LOOK_DEV = 256
LOOKUPS = 8192
CAP = 64
N_DP = 4
N_SHARD = 8


def place_ends(array, key, least, high):
    spot = [jax.random.randint(jax.random.fold_in(key, axis), (), 0, length) for axis, length in enumerate(array.shape)]
    widest = array.shape.index(max(array.shape))
    neighbour = spot[:widest] + [(spot[widest] + 1) % array.shape[widest]] + spot[widest + 1:]
    return array.at[tuple(spot)].set(least).at[tuple(neighbour)].set(high)


def levels(rng, shape, shards, smallest, top_value):
    def one(position, parts):
        heights = jax.random.uniform(jax.random.fold_in(jax.random.fold_in(rng, 6), position), (parts,), jnp.float32, smallest / len(shards), top_value / len(shards))
        return jnp.repeat(jnp.exp(heights), shape[position] // parts).reshape((-1,) + (1,) * (len(shape) - position - 1))

    factor_of = one(*shards[0])
    for cut in shards[1:]:
        factor_of = factor_of * one(*cut)
    return factor_of


def rank_bounds(count, skew):
    portions = [(1 << 20) // math.isqrt(rank ** skew) + 1 for rank in range(1, count + 1)]
    width = 1 + sum(portions) // (1 << 30)
    return np.cumsum(np.array([max(1, weight // width) for weight in portions]))


def ranked(rng, shape, count, lean):
    table = rank_bounds(count, lean)
    lot = jax.random.randint(jax.random.fold_in(rng, 1), shape, 0, int(table[count - 1]))
    grade = jnp.searchsorted(jnp.asarray(table, jnp.int32), lot, side="right")
    return jax.random.permutation(jax.random.fold_in(rng, 2), count)[grade].astype(jnp.int32)


def routed_block(stream_key, own, number, rows, number_of, top, most, skew):
    sequence = jax.random.permutation(stream_key, number_of)
    packed, common = load_shares(number_of, rows * top, most, skew, True), load_shares(number_of, rows * top, most, skew, False)
    places = jnp.arange(number_of)

    def named(tallies, turn):
        used = int((tallies > 0).sum())
        fixed = max(1, used // 4)
        shifted = fixed + (places - fixed + turn * (used - fixed)) % max(1, number_of - fixed)
        return jnp.zeros((number_of,), jnp.int32).at[sequence[jnp.where(places < fixed, places, shifted)]].set(jnp.asarray(tallies, jnp.int32))

    tallies = jnp.where(number % 4 == 0, named(packed, number // 4), named(common, number - number // 4 - 1))
    mixed = jax.random.permutation(jax.random.fold_in(own, 3), number_of)
    source_of, receiver = mixed[0:number_of // 2 * 2:2], mixed[1:number_of // 2 * 2:2]
    room = jnp.minimum(tallies[source_of] - 1, most - tallies[receiver]) // 2
    room = jnp.where((source_of == sequence[0]) | (receiver == sequence[0]) | (tallies[receiver] == 0), 0, jnp.maximum(room, 0))
    shifted = jax.random.randint(jax.random.fold_in(own, 4), (number_of // 2,), 0, 1 << 20) % (room + 1)
    tallies = tallies.at[source_of].add(-shifted).at[receiver].add(shifted)
    items = jnp.searchsorted(jnp.cumsum(tallies), jnp.arange(rows * top), side="right").astype(jnp.int32)
    listing = items.reshape(top, rows).T
    listing = listing[jax.random.permutation(jax.random.fold_in(own, 1), rows)]
    turn = jax.random.randint(jax.random.fold_in(own, 2), (rows, 1), 0, top)
    return jnp.take_along_axis(listing, (jnp.arange(top)[None, :] + turn) % top, axis=1)


def load_shares(count, total, reach, lean, full):
    portions = [(1 << 20) // math.isqrt(grade ** lean) + 1 for grade in range(1, count + 1)]
    largest = reach if full else min(reach, max(-(-total // count), total * portions[0] // sum(portions)))
    least = 1 if total - largest >= count - 1 else 0
    counts, rest = [largest] + [least] * (count - 1), total - largest - least * (count - 1)
    while rest > 0:
        candidates = [i for i in range(1, count) if counts[i] < largest] or [i for i in range(1, count) if counts[i] < reach]
        mass, left = sum([portions[i] for i in candidates]), rest
        for i in candidates:
            extra = min(reach - counts[i], max(1, left * portions[i] // mass), rest)
            counts[i] = counts[i] + extra
            rest = rest - extra
    return np.array(counts)


def centred(key, extent, spread, limit, shards=(), kind=jnp.bfloat16):
    result = jax.random.normal(key, extent, jnp.float32) * spread
    if len(shards) > 0:
        result = levels(key, extent, shards, -0.22, 0.18) * result
    return jnp.clip(result, min=-limit, max=limit).astype(kind)


def setup_inputs(seed: int = 0) -> dict:
    seeds = jax.random.split(jax.random.key(seed), 10)
    hot_ids = place_ends(ranked(seeds[0], (SAMPLES, L_HOT), HOT, 2), jax.random.fold_in(seeds[0], 3), 0, HOT - 1).astype(jnp.int32)
    cold_owner_keys = jax.random.split(jax.random.fold_in(seeds[1], 1), LOOKUPS // LOOK_DEV)
    cold_owner_turns = jax.random.permutation(jax.random.fold_in(seeds[1], 3), LOOKUPS // LOOK_DEV)
    cold_owner = jax.vmap(lambda own, number: routed_block(jax.random.fold_in(seeds[1], 2), own, number, LOOK_DEV, N_SHARD, 1, CAP, 2))(cold_owner_keys, cold_owner_turns).reshape((LOOKUPS, 1))
    cold_offset = place_ends(jax.random.randint(seeds[2], (LOOKUPS,), 0, COLD_DEV), jax.random.fold_in(seeds[2], 1), 0, COLD_DEV - 1).astype(jnp.int32)
    hot_table = centred(seeds[3], (HOT, E), 0.35, 2.0)
    cold_table = centred(seeds[4], (COLD, E), 0.7, 4.0, ((0, 8),))
    w_in = centred(seeds[5], (D_IN, H), D_IN ** -0.5, 0.375, ((1, 8),))
    bias_in = jnp.clip(jax.random.uniform(seeds[6], (1, H), jnp.float32, -0.59765625, 0.59765625) * levels(seeds[6], (1, H), ((1, 8),), -0.4, 0.0), -0.59765625, 0.59765625).astype(jnp.bfloat16)
    w_out = centred(seeds[7], (1, H), (H // 4) ** -0.5, 0.1875, ((1, 8),))
    cotangent = centred(seeds[8], (SAMPLES,), 2.0, 10.0, ((0, 32),), jnp.float32)
    return dict(hot_ids=hot_ids, cold_owner=cold_owner, cold_offset=cold_offset, hot_table=hot_table, cold_table=cold_table, w_in=w_in, bias_in=bias_in, w_out=w_out, cotangent=cotangent)


def round_keep(value):
    return lax.optimization_barrier(value.astype(jnp.bfloat16)).astype(jnp.float32)


def reference(hot_ids, cold_owner, cold_offset, hot_table, cold_table, w_in, bias_in, w_out, cotangent):
    members = B_DEV * N_SHARD
    cold_row = (cold_owner[:, 0] * COLD_DEV + cold_offset).astype(jnp.int32)
    hot_blocks = hot_ids.reshape(N_DP, members, L_HOT)
    cold_blocks = cold_row.reshape(N_DP, members * L_COLD)
    cot_blocks = cotangent.reshape(N_DP, members)
    head = w_out[0].astype(jnp.float32)
    bias_row = bias_in[0].astype(jnp.float32)

    def one_group(running, by_group):
        weight_sum, hot_sum, cold_sum = running
        hot_block, cold_block, group_cot = by_group
        hot_pooled = jnp.sum(hot_table[hot_block].astype(jnp.float32), axis=1)
        cold_pooled = jnp.sum(cold_table[cold_block].astype(jnp.float32).reshape(members, L_COLD, E), axis=1)
        inputs = jnp.concatenate([hot_pooled, cold_pooled], axis=1).astype(jnp.bfloat16)
        preact = jnp.dot(inputs, w_in, preferred_element_type=jnp.float32) + bias_row[None, :]
        sigma = jax.nn.sigmoid(preact)
        hidden = (preact * sigma).astype(jnp.bfloat16)
        logit_block = jnp.dot(hidden, w_out[0], preferred_element_type=jnp.float32)
        slope = sigma * (1.0 + preact * (1.0 - sigma))
        hidden_grad = (group_cot[:, None] * head[None, :] * slope).astype(jnp.bfloat16)
        input_grad = jnp.dot(hidden_grad, w_in.T, preferred_element_type=jnp.float32).astype(jnp.bfloat16)
        weight_part = jnp.dot(inputs.T, hidden_grad, preferred_element_type=jnp.float32)
        hot_rows_grad = jnp.repeat(input_grad[:, :E].astype(jnp.float32), L_HOT, axis=0)
        cold_rows_grad = jnp.repeat(input_grad[:, E:].astype(jnp.float32), L_COLD, axis=0)
        hot_next = hot_sum.at[hot_block.reshape(-1)].add(hot_rows_grad)
        cold_part = jnp.zeros((COLD, E), jnp.float32).at[cold_block].add(cold_rows_grad)
        updated = (weight_sum + round_keep(weight_part), hot_next, cold_sum + round_keep(cold_part))
        return updated, logit_block

    initial = (jnp.zeros((D_IN, H), jnp.float32), jnp.zeros((HOT, E), jnp.float32), jnp.zeros((COLD, E), jnp.float32))
    finals, logit_blocks = lax.scan(one_group, initial, (hot_blocks, cold_blocks, cot_blocks))
    weight_sum, hot_sum, cold_sum = finals
    return logit_blocks.reshape(SAMPLES), hot_sum.astype(jnp.bfloat16), cold_sum.astype(jnp.bfloat16), weight_sum
```

```python
import functools

import jax
import jax.numpy as jnp
from jax import lax
from jax.experimental import pallas as pl
from jax.experimental.pallas import tpu as pltpu
from jax.sharding import PartitionSpec as P

F32, BF16, I32 = jnp.float32, jnp.bfloat16, jnp.int32
IDS, COT, HOTIN, ROWS, COLDIN, PART, LOGIT, COLDG, HOTG = range(9)
DIDS, DWEIGHT, DHOT, DCOLD = range(4)


def dot(a, b):
    return jnp.dot(a, b, preferred_element_type=F32)


def dot_nt(a, b):
    return lax.dot_general(a, b, (((1,), (1,)), ((), ())), preferred_element_type=F32)


def dot_tn(a, b):
    return lax.dot_general(a, b, (((0,), (0,)), ((), ())), preferred_element_type=F32)


def kernel(
    n, groups, cap, keep_all,
    ids_ref, hot_col, cot_ref, hot_table, cold_table, w_in, bias, w_out,
    logit_out, hot_out, cold_out, weight_out,
    idg, cotg, ing, hot_src, cold_src, pick, tri, offc, onehot, rows_src, answer,
    hot_counts, grads, part_src, part_in, logit_src, logit_in, slot_src, slot_in,
    hotg_src, hotg_in, weight_in, hot_in, gacc,
    ssem, rsem, dssem, drsem,
):
    me = lax.axis_index("shard")
    mine = lax.axis_index("dp")
    samples, width = hot_col.shape
    table_rows, embed = hot_table.shape
    owned = cold_table.shape[0]
    hidden_dev = w_in.shape[1]
    kept = hot_out.shape[0]
    group = n * samples
    slots = n * cap

    def shard_copy(phase, src, dst, peer, source):
        return pltpu.make_async_remote_copy(
            src_ref=src, dst_ref=dst, send_sem=ssem.at[phase, peer], recv_sem=rsem.at[phase, source],
            device_id={"shard": peer}, device_id_type=pl.DeviceIdType.MESH,
        )

    def dp_copy(phase, src, dst, peer, source):
        return pltpu.make_async_remote_copy(
            src_ref=src, dst_ref=dst, send_sem=dssem.at[phase, peer], recv_sem=drsem.at[phase, source],
            device_id={"dp": peer}, device_id_type=pl.DeviceIdType.MESH,
        )

    def peers(body, count=n, own=None):
        own = me if own is None else own

        def step(i, carry):
            body(lax.rem(own + count - i, count))
            return carry

        lax.fori_loop(1, count, step, 0)

    def dp_peers(body):
        peers(body, groups, mine)

    barrier = pltpu.get_barrier_semaphore()
    peers(lambda j: pl.semaphore_signal(
        barrier, inc=1, device_id={"shard": j}, device_id_type=pl.DeviceIdType.MESH))
    dp_peers(lambda j: pl.semaphore_signal(
        barrier, inc=1, device_id={"dp": j}, device_id_type=pl.DeviceIdType.MESH))
    pl.semaphore_wait(barrier, n - 1 + groups - 1)

    def send_ids(j):
        shard_copy(IDS, ids_ref, idg.at[mine, me], j, me).start()
        shard_copy(COT, cot_ref, cotg.at[me], j, me).start()

    peers(send_ids)
    idg[mine, me] = ids_ref[...]
    cotg[me] = cot_ref[...]

    chunk = min(512, table_rows)
    pooled = jnp.zeros((samples, embed), F32)
    lane = lax.broadcasted_iota(I32, (samples, chunk), 1)
    for c in range(table_rows // chunk):
        count = jnp.zeros((samples, chunk), F32)
        for k in range(width):
            count = count + jnp.where(hot_col[:, k : k + 1] - c * chunk == lane, 1.0, 0.0)
        pooled = pooled + dot(count.astype(BF16), hot_table[c * chunk : (c + 1) * chunk, :])
    hot_src[...] = pooled.astype(BF16)
    peers(lambda j: shard_copy(HOTIN, hot_src, ing.at[me, :, pl.ds(0, embed)], j, me).start())
    ing[me, :, 0:embed] = hot_src[...]

    lookups = 2 * samples
    row_i = lax.broadcasted_iota(I32, (lookups, lookups), 0)
    col_i = lax.broadcasted_iota(I32, (lookups, lookups), 1)
    tri[...] = jnp.where(row_i < col_i, 1.0, 0.0).astype(BF16)

    def lookup_rows(block, first):
        return jnp.concatenate([block[first : first + 1], block[first + 1 : first + 2]], axis=1)

    own_block = ids_ref[...]
    owner = lookup_rows(own_block, width)
    match = jnp.where(lax.broadcasted_iota(I32, (n, lookups), 0) == owner, 1.0, 0.0)
    order = dot(match.astype(BF16), tri[...])
    place = owner * cap + jnp.sum(match * order, axis=0, keepdims=True).astype(I32)
    slot_i = lax.broadcasted_iota(I32, (slots, samples), 0)
    pick[...] = (
        jnp.where(slot_i == place[:, :samples], 1.0, 0.0)
        + jnp.where(slot_i == place[:, samples:], 1.0, 0.0)
    ).astype(BF16)

    cap_i = lax.broadcasted_iota(I32, (cap, lookups), 0)

    def fill(d, place_at):
        def one(j, carry):
            block = idg[d, j]
            hit = jnp.where(lookup_rows(block, width) == me, 1.0, 0.0)
            spread = jnp.broadcast_to(hit, (16, lookups))
            position = dot(spread.astype(BF16), tri[...])[0:1].astype(I32)
            chosen = jnp.where(cap_i == position, hit, 0.0).astype(BF16)
            offset = lookup_rows(block, width + 2)
            high = jnp.broadcast_to((offset >> 6).astype(F32), (embed, lookups)).astype(BF16)
            low = jnp.broadcast_to((offset & 63).astype(F32), (embed, lookups)).astype(BF16)
            found = dot_nt(chosen, high) * 64.0 + dot_nt(chosen, low)
            offc[pl.ds(pl.multiple_of(j * cap, cap), cap), :] = found.astype(I32)
            return carry

        lax.fori_loop(0, n, one, 0)
        lanes = lax.broadcasted_iota(I32, (slots, embed), 1)
        for c in range(owned // embed):
            onehot[place_at, :, c * embed : (c + 1) * embed] = jnp.where(
                offc[...] - c * embed == lanes, 1.0, 0.0
            ).astype(BF16)

    peers(lambda j: shard_copy(IDS, ids_ref, idg.at[mine, j], j, j).wait_recv())
    dp_peers(lambda d: dp_copy(DIDS, idg.at[mine], idg.at[mine], d, mine).start())
    at = mine if keep_all else 0
    fill(mine, at)
    rows_src[...] = dot(onehot[at], cold_table[...]).astype(BF16).reshape(n, cap, embed)
    peers(lambda j: shard_copy(ROWS, rows_src.at[j], answer.at[me], j, me).start())
    answer[me] = rows_src[me]

    kept_i = lax.broadcasted_iota(I32, (kept, samples), 0) + me * kept
    for j in range(n):
        count = jnp.zeros((kept, samples), F32)
        for k in range(width):
            count = count + jnp.where(idg[mine, j, k : k + 1, :] == kept_i, 1.0, 0.0)
        hot_counts[:, j * samples : (j + 1) * samples] = count.astype(BF16)

    peers(lambda j: shard_copy(ROWS, rows_src.at[j], answer.at[j], j, j).wait_recv())
    cold_src[...] = dot_tn(pick[...], answer[...].reshape(slots, embed)).astype(BF16)
    peers(lambda j: shard_copy(COLDIN, cold_src, ing.at[me, :, pl.ds(embed, embed)], j, me).start())
    ing[me, :, embed : 2 * embed] = cold_src[...]

    head_rows = jnp.broadcast_to(w_out[...], (16, hidden_dev))

    def dense(i, carry):
        j = lax.rem(me + i, n)

        @pl.when(i > 0)
        def _():
            shard_copy(HOTIN, hot_src, ing.at[j, :, pl.ds(0, embed)], j, j).wait_recv()
            shard_copy(COLDIN, cold_src, ing.at[j, :, pl.ds(embed, embed)], j, j).wait_recv()
            shard_copy(COT, cot_ref, cotg.at[j], j, j).wait_recv()

        pre = dot(ing[j], w_in[...]) + bias[...].astype(F32)
        sigma = jax.nn.sigmoid(pre)
        hidden = (pre * sigma).astype(BF16)
        logit_src[j] = dot_nt(head_rows, hidden)[0:8]
        cot = jnp.broadcast_to(cotg[j][0:1], (samples, samples)).T
        cot = jnp.concatenate([cot] * (hidden_dev // samples), axis=1)
        slope = sigma * (1.0 + pre * (1.0 - sigma))
        grad = (cot * w_out[...].astype(F32) * slope).astype(BF16)
        grads[j] = grad
        part_src[j] = dot_nt(grad, w_in[...]).astype(BF16)

        @pl.when(i > 0)
        def _():
            shard_copy(PART, part_src.at[j], part_in.at[me], j, me).start()
            shard_copy(LOGIT, logit_src.at[j], logit_in.at[me], j, me).start()

        return carry

    lax.fori_loop(0, n, dense, 0)
    part_in[me] = part_src[me]
    logit_in[me] = logit_src[me]

    weight_in[mine] = dot_tn(
        ing[...].reshape(group, 2 * embed), grads[...].reshape(group, hidden_dev)
    ).astype(BF16)
    dp_peers(lambda d: dp_copy(DWEIGHT, weight_in.at[mine], weight_in.at[mine], d, mine).start())

    def add_part(i, total):
        j = lax.rem(me + i, n)

        @pl.when(i > 0)
        def _():
            shard_copy(PART, part_src.at[j], part_in.at[j], j, j).wait_recv()

        return total + part_in[j].astype(F32)

    total = lax.fori_loop(0, n, add_part, jnp.zeros((samples, 2 * embed), F32))
    total = total.astype(BF16)
    hotg_src[...] = total[:, 0:embed]
    slot_src[...] = dot(pick[...], total[:, embed:]).astype(BF16).reshape(n, cap, embed)

    def send_grads(j):
        shard_copy(COLDG, slot_src.at[j], slot_in.at[mine, me], j, me).start()
        shard_copy(HOTG, hotg_src, hotg_in.at[me], j, me).start()

    peers(send_grads)
    slot_in[mine, me] = slot_src[me]
    hotg_in[me] = hotg_src[...]

    dp_peers(lambda d: dp_copy(DIDS, idg.at[mine], idg.at[d], d, d).wait_recv())
    if keep_all:
        dp_peers(lambda d: fill(d, d))

    peers(lambda j: shard_copy(COLDG, slot_src.at[j], slot_in.at[mine, j], j, j).wait_recv())
    dp_peers(lambda d: dp_copy(DCOLD, slot_in.at[mine], slot_in.at[mine], d, mine).start())
    peers(lambda j: shard_copy(HOTG, hotg_src, hotg_in.at[j], j, j).wait_recv())
    hot_in[mine] = dot(hot_counts[...], hotg_in[...].reshape(group, embed)).astype(BF16)
    dp_peers(lambda d: dp_copy(DHOT, hot_in.at[mine], hot_in.at[mine], d, mine).start())

    def add_cold(d):
        where = d
        if not keep_all:
            fill(d, 0)
            where = 0
        gacc[...] += dot_tn(slot_in[d].reshape(slots, embed), onehot[where])

    gacc[...] = jnp.zeros_like(gacc)
    add_cold(mine)

    logits = jnp.zeros((8, samples), F32)

    def add_logit(i, total):
        j = lax.rem(me + i, n)

        @pl.when(i > 0)
        def _():
            shard_copy(LOGIT, logit_src.at[j], logit_in.at[j], j, j).wait_recv()

        return total + logit_in[j]

    logit_out[...] = lax.fori_loop(0, n, add_logit, logits)

    weight_out[...] = weight_in[mine].astype(F32)

    def add_weight(d):
        dp_copy(DWEIGHT, weight_in.at[mine], weight_in.at[d], d, d).wait_recv()
        weight_out[...] += weight_in[d].astype(F32)

    dp_peers(add_weight)

    def cold_from(d):
        dp_copy(DCOLD, slot_in.at[mine], slot_in.at[d], d, d).wait_recv()
        add_cold(d)

    dp_peers(cold_from)
    cold_out[...] = gacc[...].T.astype(BF16)

    def hot_from(i, total):
        d = lax.rem(mine + i, groups)

        @pl.when(i > 0)
        def _():
            dp_copy(DHOT, hot_in.at[mine], hot_in.at[d], d, d).wait_recv()

        return total + hot_in[d].astype(F32)

    hot_out[...] = lax.fori_loop(0, groups, hot_from, jnp.zeros((kept, embed), F32)).astype(BF16)

    def sent(j):
        shard_copy(IDS, ids_ref, idg.at[mine, me], j, me).wait_send()
        shard_copy(COT, cot_ref, cotg.at[me], j, me).wait_send()
        shard_copy(HOTIN, hot_src, ing.at[me, :, pl.ds(0, embed)], j, me).wait_send()
        shard_copy(ROWS, rows_src.at[j], answer.at[me], j, me).wait_send()
        shard_copy(COLDIN, cold_src, ing.at[me, :, pl.ds(embed, embed)], j, me).wait_send()
        shard_copy(PART, part_src.at[j], part_in.at[me], j, me).wait_send()
        shard_copy(LOGIT, logit_src.at[j], logit_in.at[me], j, me).wait_send()
        shard_copy(COLDG, slot_src.at[j], slot_in.at[mine, me], j, me).wait_send()
        shard_copy(HOTG, hotg_src, hotg_in.at[me], j, me).wait_send()

    peers(sent)

    def dp_sent(d):
        dp_copy(DIDS, idg.at[mine], idg.at[mine], d, mine).wait_send()
        dp_copy(DWEIGHT, weight_in.at[mine], weight_in.at[mine], d, mine).wait_send()
        dp_copy(DCOLD, slot_in.at[mine], slot_in.at[mine], d, mine).wait_send()
        dp_copy(DHOT, hot_in.at[mine], hot_in.at[mine], d, mine).wait_send()

    dp_peers(dp_sent)


def shards(
    hot_ids, cold_owner, cold_offset, hot_table, cold_table, w_in, bias_in, w_out, cotangent
):
    n = lax.axis_size("shard")
    groups = lax.axis_size("dp")
    samples, width = hot_ids.shape
    table_rows, embed = hot_table.shape
    owned = cold_table.shape[0]
    inputs_dim, hidden_dev = w_in.shape
    lookups = cold_offset.shape[0]
    cap = max(16, 2 * lookups // n)
    kept = table_rows // n
    slots = n * cap
    keep_all = groups * slots * owned * 2 <= 20 * 2**20
    owner_rows = cold_owner.reshape(samples, 2).T
    offset_rows = cold_offset.reshape(samples, 2).T
    ids = jnp.concatenate(
        [hot_ids.T, owner_rows, offset_rows, jnp.zeros((12 - width, samples), I32)], axis=0
    )
    cot = jnp.broadcast_to(cotangent[None, :], (8, samples))
    vmem = pl.BlockSpec(memory_space=pltpu.VMEM)
    logits, hot, cold, weight = pl.pallas_call(
        functools.partial(kernel, n, groups, cap, keep_all),
        out_shape=(
            jax.ShapeDtypeStruct((8, samples), F32),
            jax.ShapeDtypeStruct((kept, embed), BF16),
            jax.ShapeDtypeStruct((owned, embed), BF16),
            jax.ShapeDtypeStruct((inputs_dim, hidden_dev), F32),
        ),
        in_specs=[vmem] * 8,
        out_specs=(vmem,) * 4,
        scratch_shapes=[
            pltpu.VMEM((groups, n, 16, samples), I32),
            pltpu.VMEM((n, 8, samples), F32),
            pltpu.VMEM((n, samples, 2 * embed), BF16),
            pltpu.VMEM((samples, embed), BF16),
            pltpu.VMEM((samples, embed), BF16),
            pltpu.VMEM((slots, samples), BF16),
            pltpu.VMEM((lookups, lookups), BF16),
            pltpu.VMEM((slots, embed), I32),
            pltpu.VMEM((groups if keep_all else 1, slots, owned), BF16),
            pltpu.VMEM((n, cap, embed), BF16),
            pltpu.VMEM((n, cap, embed), BF16),
            pltpu.VMEM((kept, n * samples), BF16),
            pltpu.VMEM((n, samples, hidden_dev), BF16),
            pltpu.VMEM((n, samples, 2 * embed), BF16),
            pltpu.VMEM((n, samples, 2 * embed), BF16),
            pltpu.VMEM((n, 8, samples), F32),
            pltpu.VMEM((n, 8, samples), F32),
            pltpu.VMEM((n, cap, embed), BF16),
            pltpu.VMEM((groups, n, cap, embed), BF16),
            pltpu.VMEM((samples, embed), BF16),
            pltpu.VMEM((n, samples, embed), BF16),
            pltpu.VMEM((groups, inputs_dim, hidden_dev), BF16),
            pltpu.VMEM((groups, kept, embed), BF16),
            pltpu.VMEM((embed, owned), F32),
            pltpu.SemaphoreType.DMA((9, n)),
            pltpu.SemaphoreType.DMA((9, n)),
            pltpu.SemaphoreType.DMA((4, groups)),
            pltpu.SemaphoreType.DMA((4, groups)),
        ],
        compiler_params=pltpu.CompilerParams(
            collective_id=0, has_side_effects=True, vmem_limit_bytes=56 * 2**20
        ),
    )(ids, hot_ids, cot, hot_table, cold_table, w_in, bias_in, w_out)
    return (logits[0], hot, cold, weight)


def solution(mesh):
    in_specs = (
        P(("dp", "shard"), None),
        P(("dp", "shard"), None),
        P(("dp", "shard")),
        P(),
        P("shard", None),
        P(None, "shard"),
        P(None, "shard"),
        P(None, "shard"),
        P(("dp", "shard")),
    )
    out_specs = (P(("dp", "shard")), P("shard", None), P("shard", None), P(None, "shard"))
    return jax.shard_map(shards, mesh=mesh, in_specs=in_specs, out_specs=out_specs, check_vma=False)
```

```python
import functools

import jax
import jax.numpy as jnp
from jax import lax
from jax.experimental import pallas as pl
from jax.experimental.pallas import tpu as pltpu
from jax.sharding import PartitionSpec as P

F32, BF16, I32 = jnp.float32, jnp.bfloat16, jnp.int32
IDS, COT, HOTIN, ROWS, COLDIN, PART, LOGIT, COLDG, HOTG = range(9)
DIDS, DWEIGHT, DHOT, DCOLD = range(4)


def dot(a, b):
    return jnp.dot(a, b, preferred_element_type=F32)


def dot_nt(a, b):
    return lax.dot_general(a, b, (((1,), (1,)), ((), ())), preferred_element_type=F32)


def dot_tn(a, b):
    return lax.dot_general(a, b, (((0,), (0,)), ((), ())), preferred_element_type=F32)


def kernel(
    n, groups, cap, keep_all,
    hot_rows, owner_ref, offset_ref, cot_row, hot_table, cold_table, w_in, bias, w_out,
    logit_out, hot_out, cold_out, weight_out,
    ids_ref, cot_ref, hot_col, idg, cotg, ing, hot_src, cold_src, pick, tri, offc, onehot, turned,
    rows_src, answer,
    hot_counts, grads, part_src, part_in, logit_src, logit_in, slot_src, slot_in,
    hotg_src, hotg_in, weight_in, hot_in, gacc,
    ssem, rsem, dssem, drsem,
):
    me = lax.axis_index("shard")
    mine = lax.axis_index("dp")
    width, samples = hot_rows.shape
    table_rows, embed = hot_table.shape
    owned = cold_table.shape[0]
    hidden_dev = w_in.shape[1]
    kept = hot_out.shape[0]
    group = n * samples
    slots = n * cap

    def shard_copy(phase, src, dst, peer, source):
        return pltpu.make_async_remote_copy(
            src_ref=src, dst_ref=dst, send_sem=ssem.at[phase, peer], recv_sem=rsem.at[phase, source],
            device_id={"shard": peer}, device_id_type=pl.DeviceIdType.MESH,
        )

    def dp_copy(phase, src, dst, peer, source):
        return pltpu.make_async_remote_copy(
            src_ref=src, dst_ref=dst, send_sem=dssem.at[phase, peer], recv_sem=drsem.at[phase, source],
            device_id={"dp": peer}, device_id_type=pl.DeviceIdType.MESH,
        )

    def peers(body, count=n, own=None):
        own = me if own is None else own

        def step(i, carry):
            body(lax.rem(own + count - i, count))
            return carry

        lax.fori_loop(1, count, step, 0)

    def dp_peers(body):
        peers(body, groups, mine)

    ids_ref[0:width] = hot_rows[...]
    ids_ref[width : width + 2] = owner_ref[...]
    ids_ref[width + 2 : width + 4] = offset_ref[...]
    ids_ref[width + 4 : 16] = jnp.zeros((12 - width, samples), I32)
    cot_ref[...] = jnp.broadcast_to(cot_row[...], (8, samples))

    barrier = pltpu.get_barrier_semaphore()
    peers(lambda j: pl.semaphore_signal(
        barrier, inc=1, device_id={"shard": j}, device_id_type=pl.DeviceIdType.MESH))
    dp_peers(lambda j: pl.semaphore_signal(
        barrier, inc=1, device_id={"dp": j}, device_id_type=pl.DeviceIdType.MESH))
    pl.semaphore_wait(barrier, n - 1 + groups - 1)

    def send_ids(j):
        shard_copy(IDS, ids_ref, idg.at[mine, me], j, me).start()
        shard_copy(COT, cot_ref, cotg.at[me], j, me).start()

    peers(send_ids)
    idg[mine, me] = ids_ref[...]
    cotg[me] = cot_ref[...]

    spare = jnp.zeros((samples - width, samples), F32)
    hot_col[...] = jnp.concatenate([hot_rows[...].astype(F32), spare], axis=0).T.astype(I32)
    chunk = min(512, table_rows)
    pooled = jnp.zeros((samples, embed), F32)
    lane = lax.broadcasted_iota(I32, (samples, chunk), 1)
    for c in range(table_rows // chunk):
        count = jnp.zeros((samples, chunk), F32)
        for k in range(width):
            count = count + jnp.where(hot_col[:, k : k + 1] - c * chunk == lane, 1.0, 0.0)
        pooled = pooled + dot(count.astype(BF16), hot_table[c * chunk : (c + 1) * chunk, :])
    hot_src[...] = pooled.astype(BF16)
    peers(lambda j: shard_copy(HOTIN, hot_src, ing.at[me, :, pl.ds(0, embed)], j, me).start())
    ing[me, :, 0:embed] = hot_src[...]

    lookups = 2 * samples
    row_i = lax.broadcasted_iota(I32, (lookups, lookups), 0)
    col_i = lax.broadcasted_iota(I32, (lookups, lookups), 1)
    tri[...] = jnp.where(row_i < col_i, 1.0, 0.0).astype(BF16)

    def lookup_rows(block, first):
        return jnp.concatenate([block[first : first + 1], block[first + 1 : first + 2]], axis=1)

    own_block = ids_ref[...]
    owner = lookup_rows(own_block, width)
    match = jnp.where(lax.broadcasted_iota(I32, (n, lookups), 0) == owner, 1.0, 0.0)
    order = dot(match.astype(BF16), tri[...])
    place = owner * cap + jnp.sum(match * order, axis=0, keepdims=True).astype(I32)
    slot_i = lax.broadcasted_iota(I32, (slots, lookups), 0)
    first = 2 * lax.broadcasted_iota(I32, (lookups, samples), 1)
    lookup_i = lax.broadcasted_iota(I32, (lookups, samples), 0)
    pair = jnp.where((lookup_i == first) | (lookup_i == first + 1), 1.0, 0.0).astype(BF16)
    pick[...] = dot(jnp.where(slot_i == place, 1.0, 0.0).astype(BF16), pair).astype(BF16)

    cap_i = lax.broadcasted_iota(I32, (cap, lookups), 0)

    def find(d):
        hits = [jnp.where(lookup_rows(idg[d, j], width) == me, 1.0, 0.0) for j in range(n)]
        positions = dot(jnp.concatenate(hits, axis=0).astype(BF16), tri[...]).astype(I32)
        for j in range(n):
            chosen = jnp.where(cap_i == positions[j : j + 1], hits[j], 0.0).astype(BF16)
            offset = lookup_rows(idg[d, j], width + 2)
            high = jnp.broadcast_to((offset >> 6).astype(F32), (embed, lookups)).astype(BF16)
            low = jnp.broadcast_to((offset & 63).astype(F32), (embed, lookups)).astype(BF16)
            offc[j * cap : (j + 1) * cap, :] = dot_nt(chosen, high) * 64.0 + dot_nt(chosen, low)

    tall = 64

    def turn(place_at):
        row = offc[...].T[0:1].astype(I32)
        down = lax.broadcasted_iota(I32, (tall, slots), 0)
        for c in range(owned // tall):
            turned[place_at, c * tall : (c + 1) * tall, :] = jnp.where(
                row - c * tall == down, 1.0, 0.0
            ).astype(BF16)

    peers(lambda j: shard_copy(IDS, ids_ref, idg.at[mine, j], j, j).wait_recv())
    dp_peers(lambda d: dp_copy(DIDS, idg.at[mine], idg.at[mine], d, mine).start())
    find(mine)
    across = lax.broadcasted_iota(I32, (slots, embed), 1)
    offsets = offc[...].astype(I32)
    for c in range(owned // embed):
        onehot[:, c * embed : (c + 1) * embed] = jnp.where(
            offsets - c * embed == across, 1.0, 0.0
        ).astype(BF16)
    rows_src[...] = dot(onehot[...], cold_table[...]).astype(BF16).reshape(n, cap, embed)
    peers(lambda j: shard_copy(ROWS, rows_src.at[j], answer.at[me], j, me).start())
    answer[me] = rows_src[me]

    if keep_all:
        turn(mine)

    kept_i = lax.broadcasted_iota(I32, (kept, samples), 0) + me * kept
    for j in range(n):
        count = jnp.zeros((kept, samples), F32)
        for k in range(width):
            count = count + jnp.where(idg[mine, j, k : k + 1, :] == kept_i, 1.0, 0.0)
        hot_counts[:, j * samples : (j + 1) * samples] = count.astype(BF16)

    peers(lambda j: shard_copy(ROWS, rows_src.at[j], answer.at[j], j, j).wait_recv())
    cold_src[...] = dot_tn(pick[...], answer[...].reshape(slots, embed)).astype(BF16)
    peers(lambda j: shard_copy(COLDIN, cold_src, ing.at[me, :, pl.ds(embed, embed)], j, me).start())
    ing[me, :, embed : 2 * embed] = cold_src[...]

    def other_tables(low, high):
        def step(i, carry):
            d = lax.rem(mine + groups - i, groups)
            dp_copy(DIDS, idg.at[mine], idg.at[d], d, d).wait_recv()
            if keep_all:
                find(d)
                turn(d)
            return carry

        lax.fori_loop(low, high, step, 0)

    half = 1 + groups // 2
    other_tables(1, half)

    head_rows = jnp.broadcast_to(w_out[...], (16, hidden_dev))

    def dense(i, carry):
        j = lax.rem(me + i, n)

        @pl.when(i > 0)
        def _():
            shard_copy(HOTIN, hot_src, ing.at[j, :, pl.ds(0, embed)], j, j).wait_recv()
            shard_copy(COLDIN, cold_src, ing.at[j, :, pl.ds(embed, embed)], j, j).wait_recv()
            shard_copy(COT, cot_ref, cotg.at[j], j, j).wait_recv()

        pre = dot(ing[j], w_in[...]) + bias[...].astype(F32)
        sigma = jax.nn.sigmoid(pre)
        hidden = (pre * sigma).astype(BF16)
        logit_src[j] = dot_nt(head_rows, hidden)[0:8]
        cot = jnp.broadcast_to(cotg[j][0:1], (samples, samples)).T
        cot = jnp.concatenate([cot] * (hidden_dev // samples), axis=1)
        slope = sigma * (1.0 + pre * (1.0 - sigma))
        grad = (cot * w_out[...].astype(F32) * slope).astype(BF16)
        grads[j] = grad
        part_src[j] = dot_nt(grad, w_in[...]).astype(BF16)

        @pl.when(i > 0)
        def _():
            shard_copy(PART, part_src.at[j], part_in.at[me], j, me).start()
            shard_copy(LOGIT, logit_src.at[j], logit_in.at[me], j, me).start()

        return carry

    lax.fori_loop(0, n, dense, 0)
    part_in[me] = part_src[me]
    logit_in[me] = logit_src[me]

    weight_in[mine] = dot_tn(
        ing[...].reshape(group, 2 * embed), grads[...].reshape(group, hidden_dev)
    ).astype(BF16)
    dp_peers(lambda d: dp_copy(DWEIGHT, weight_in.at[mine], weight_in.at[mine], d, mine).start())

    other_tables(half, groups)

    def add_part(i, total):
        j = lax.rem(me + i, n)

        @pl.when(i > 0)
        def _():
            shard_copy(PART, part_src.at[j], part_in.at[j], j, j).wait_recv()

        return total + part_in[j].astype(F32)

    total = lax.fori_loop(0, n, add_part, jnp.zeros((samples, 2 * embed), F32))
    total = total.astype(BF16)
    hotg_src[...] = total[:, 0:embed]
    slot_src[...] = dot(pick[...], total[:, embed:]).astype(BF16).reshape(n, cap, embed)

    def send_grads(j):
        shard_copy(COLDG, slot_src.at[j], slot_in.at[mine, me], j, me).start()
        shard_copy(HOTG, hotg_src, hotg_in.at[me], j, me).start()

    peers(send_grads)
    slot_in[mine, me] = slot_src[me]
    hotg_in[me] = hotg_src[...]

    peers(lambda j: shard_copy(COLDG, slot_src.at[j], slot_in.at[mine, j], j, j).wait_recv())
    dp_peers(lambda d: dp_copy(DCOLD, slot_in.at[mine], slot_in.at[mine], d, mine).start())
    peers(lambda j: shard_copy(HOTG, hotg_src, hotg_in.at[j], j, j).wait_recv())
    hot_in[mine] = dot(hot_counts[...], hotg_in[...].reshape(group, embed)).astype(BF16)
    dp_peers(lambda d: dp_copy(DHOT, hot_in.at[mine], hot_in.at[mine], d, mine).start())

    def add_cold(d):
        where = d
        if not keep_all:
            find(d)
            turn(0)
            where = 0
        gacc[...] += dot(turned[where], slot_in[d].reshape(slots, embed))

    gacc[...] = jnp.zeros_like(gacc)
    add_cold(mine)

    logits = jnp.zeros((8, samples), F32)

    def add_logit(i, total):
        j = lax.rem(me + i, n)

        @pl.when(i > 0)
        def _():
            shard_copy(LOGIT, logit_src.at[j], logit_in.at[j], j, j).wait_recv()

        return total + logit_in[j]

    logit_out[...] = lax.fori_loop(0, n, add_logit, logits)[0:1]

    weight_out[...] = weight_in[mine].astype(F32)

    def add_weight(d):
        dp_copy(DWEIGHT, weight_in.at[mine], weight_in.at[d], d, d).wait_recv()
        weight_out[...] += weight_in[d].astype(F32)

    dp_peers(add_weight)

    def cold_from(d):
        dp_copy(DCOLD, slot_in.at[mine], slot_in.at[d], d, d).wait_recv()
        add_cold(d)

    dp_peers(cold_from)
    cold_out[...] = gacc[...].astype(BF16)

    def hot_from(i, total):
        d = lax.rem(mine + i, groups)

        @pl.when(i > 0)
        def _():
            dp_copy(DHOT, hot_in.at[mine], hot_in.at[d], d, d).wait_recv()

        return total + hot_in[d].astype(F32)

    hot_out[...] = lax.fori_loop(0, groups, hot_from, jnp.zeros((kept, embed), F32)).astype(BF16)

    def sent(j):
        shard_copy(IDS, ids_ref, idg.at[mine, me], j, me).wait_send()
        shard_copy(COT, cot_ref, cotg.at[me], j, me).wait_send()
        shard_copy(HOTIN, hot_src, ing.at[me, :, pl.ds(0, embed)], j, me).wait_send()
        shard_copy(ROWS, rows_src.at[j], answer.at[me], j, me).wait_send()
        shard_copy(COLDIN, cold_src, ing.at[me, :, pl.ds(embed, embed)], j, me).wait_send()
        shard_copy(PART, part_src.at[j], part_in.at[me], j, me).wait_send()
        shard_copy(LOGIT, logit_src.at[j], logit_in.at[me], j, me).wait_send()
        shard_copy(COLDG, slot_src.at[j], slot_in.at[mine, me], j, me).wait_send()
        shard_copy(HOTG, hotg_src, hotg_in.at[me], j, me).wait_send()

    peers(sent)

    def dp_sent(d):
        dp_copy(DIDS, idg.at[mine], idg.at[mine], d, mine).wait_send()
        dp_copy(DWEIGHT, weight_in.at[mine], weight_in.at[mine], d, mine).wait_send()
        dp_copy(DCOLD, slot_in.at[mine], slot_in.at[mine], d, mine).wait_send()
        dp_copy(DHOT, hot_in.at[mine], hot_in.at[mine], d, mine).wait_send()

    dp_peers(dp_sent)


def shards(
    hot_ids, cold_owner, cold_offset, hot_table, cold_table, w_in, bias_in, w_out, cotangent
):
    n = lax.axis_size("shard")
    groups = lax.axis_size("dp")
    samples = hot_ids.shape[0]
    table_rows, embed = hot_table.shape
    owned = cold_table.shape[0]
    inputs_dim, hidden_dev = w_in.shape
    lookups = cold_offset.shape[0]
    cap = max(16, 2 * lookups // n)
    kept = table_rows // n
    slots = n * cap
    keep_all = groups * slots * owned * 2 <= 20 * 2**20
    vmem = pl.BlockSpec(memory_space=pltpu.VMEM)
    logits, hot, cold, weight = pl.pallas_call(
        functools.partial(kernel, n, groups, cap, keep_all),
        out_shape=(
            jax.ShapeDtypeStruct((1, samples), F32),
            jax.ShapeDtypeStruct((kept, embed), BF16),
            jax.ShapeDtypeStruct((owned, embed), BF16),
            jax.ShapeDtypeStruct((inputs_dim, hidden_dev), F32),
        ),
        in_specs=[vmem] * 9,
        out_specs=(vmem,) * 4,
        scratch_shapes=[
            pltpu.VMEM((16, samples), I32),
            pltpu.VMEM((8, samples), F32),
            pltpu.VMEM((samples, samples), I32),
            pltpu.VMEM((groups, n, 16, samples), I32),
            pltpu.VMEM((n, 8, samples), F32),
            pltpu.VMEM((n, samples, 2 * embed), BF16),
            pltpu.VMEM((samples, embed), BF16),
            pltpu.VMEM((samples, embed), BF16),
            pltpu.VMEM((slots, samples), BF16),
            pltpu.VMEM((lookups, lookups), BF16),
            pltpu.VMEM((slots, embed), F32),
            pltpu.VMEM((slots, owned), BF16),
            pltpu.VMEM((groups if keep_all else 1, owned, slots), BF16),
            pltpu.VMEM((n, cap, embed), BF16),
            pltpu.VMEM((n, cap, embed), BF16),
            pltpu.VMEM((kept, n * samples), BF16),
            pltpu.VMEM((n, samples, hidden_dev), BF16),
            pltpu.VMEM((n, samples, 2 * embed), BF16),
            pltpu.VMEM((n, samples, 2 * embed), BF16),
            pltpu.VMEM((n, 8, samples), F32),
            pltpu.VMEM((n, 8, samples), F32),
            pltpu.VMEM((n, cap, embed), BF16),
            pltpu.VMEM((groups, n, cap, embed), BF16),
            pltpu.VMEM((samples, embed), BF16),
            pltpu.VMEM((n, samples, embed), BF16),
            pltpu.VMEM((groups, inputs_dim, hidden_dev), BF16),
            pltpu.VMEM((groups, kept, embed), BF16),
            pltpu.VMEM((owned, embed), F32),
            pltpu.SemaphoreType.DMA((9, n)),
            pltpu.SemaphoreType.DMA((9, n)),
            pltpu.SemaphoreType.DMA((4, groups)),
            pltpu.SemaphoreType.DMA((4, groups)),
        ],
        compiler_params=pltpu.CompilerParams(
            collective_id=0, has_side_effects=True, vmem_limit_bytes=56 * 2**20
        ),
    )(
        hot_ids.T, cold_owner.reshape(2, samples), cold_offset.reshape(2, samples),
        cotangent.reshape(1, samples), hot_table, cold_table, w_in, bias_in, w_out,
    )
    return (logits.reshape(samples), hot, cold, weight)


def solution(mesh):
    in_specs = (
        P(("dp", "shard"), None),
        P(("dp", "shard"), None),
        P(("dp", "shard")),
        P(),
        P("shard", None),
        P(None, "shard"),
        P(None, "shard"),
        P(None, "shard"),
        P(("dp", "shard")),
    )
    out_specs = (P(("dp", "shard")), P("shard", None), P("shard", None), P(None, "shard"))
    return jax.shard_map(shards, mesh=mesh, in_specs=in_specs, out_specs=out_specs, check_vma=False)
```

```python
import functools

import jax
import jax.numpy as jnp
from jax import lax
from jax.experimental import pallas as pl
from jax.experimental.pallas import tpu as pltpu
from jax.sharding import PartitionSpec as P

F32, BF16, I32 = jnp.float32, jnp.bfloat16, jnp.int32
IDS, COT, HOTIN, ROWS, COLDIN, PART, LOGIT, COLDG, HOTG = range(9)
DIDS, DWEIGHT, DHOT, DCOLD = range(4)


def dot(a, b):
    return jnp.dot(a, b, preferred_element_type=F32)


def dot_nt(a, b):
    return lax.dot_general(a, b, (((1,), (1,)), ((), ())), preferred_element_type=F32)


def dot_tn(a, b):
    return lax.dot_general(a, b, (((0,), (0,)), ((), ())), preferred_element_type=F32)


def kernel(
    n, groups, cap, keep_all,
    hot_rows, owner_ref, offset_ref, cot_row, hot_table, cold_table, w_in, bias, w_out,
    logit_out, hot_out, cold_out, weight_out,
    ids_ref, cot_ref, hot_col, idg, cotg, ing, hot_src, cold_src, pick, tri, offc, onehot, turned,
    rows_src, answer,
    hot_counts, grads, part_src, part_in, logit_src, logit_in, slot_src, slot_in,
    hotg_src, hotg_in, weight_in, hot_in, gacc,
    ssem, rsem, dssem, drsem,
):
    me = lax.axis_index("shard")
    mine = lax.axis_index("dp")
    width, samples = hot_rows.shape
    table_rows, embed = hot_table.shape
    owned = cold_table.shape[0]
    hidden_dev = w_in.shape[1]
    kept = hot_out.shape[0]
    group = n * samples
    slots = n * cap

    def shard_copy(phase, src, dst, peer, source):
        return pltpu.make_async_remote_copy(
            src_ref=src, dst_ref=dst, send_sem=ssem.at[phase, peer], recv_sem=rsem.at[phase, source],
            device_id={"shard": peer}, device_id_type=pl.DeviceIdType.MESH,
        )

    def dp_copy(phase, src, dst, peer, source):
        return pltpu.make_async_remote_copy(
            src_ref=src, dst_ref=dst, send_sem=dssem.at[phase, peer], recv_sem=drsem.at[phase, source],
            device_id={"dp": peer}, device_id_type=pl.DeviceIdType.MESH,
        )

    def peers(body, count=n, own=None):
        own = me if own is None else own

        def step(i, carry):
            body(lax.rem(own + count - i, count))
            return carry

        lax.fori_loop(1, count, step, 0)

    def dp_peers(body):
        peers(body, groups, mine)

    sibling = me + 1 - 2 * lax.rem(me, 2)

    def same_core(body):
        def step(i, carry):
            body(lax.rem(me + n - 2 * i, n))
            return carry

        lax.fori_loop(1, n // 2, step, 0)

    def gather_start(phase, src, view):
        same_core(lambda j: shard_copy(phase, src, view(me), j, me).start())
        shard_copy(phase, src, view(me), sibling, me).start()

    def gather_pass(phase, src, view):
        def one(j):
            shard_copy(phase, src, view(j), j, j).wait_recv()
            other = j + 1 - 2 * lax.rem(j, 2)
            pltpu.make_async_remote_copy(
                src_ref=view(j), dst_ref=view(j), send_sem=ssem.at[phase, other],
                recv_sem=rsem.at[phase, j], device_id={"shard": sibling},
                device_id_type=pl.DeviceIdType.MESH,
            ).start()

        same_core(one)

    def hot_view(j):
        return ing.at[j, :, pl.ds(0, embed)]

    def cold_view(j):
        return ing.at[j, :, pl.ds(embed, embed)]

    def grad_view(j):
        return hotg_in.at[j]

    ids_ref[0:width] = hot_rows[...]
    ids_ref[width : width + 2] = owner_ref[...]
    ids_ref[width + 2 : width + 4] = offset_ref[...]
    ids_ref[width + 4 : 16] = jnp.zeros((12 - width, samples), I32)
    cot_ref[...] = jnp.broadcast_to(cot_row[...], (8, samples))

    barrier = pltpu.get_barrier_semaphore()
    peers(lambda j: pl.semaphore_signal(
        barrier, inc=1, device_id={"shard": j}, device_id_type=pl.DeviceIdType.MESH))
    dp_peers(lambda j: pl.semaphore_signal(
        barrier, inc=1, device_id={"dp": j}, device_id_type=pl.DeviceIdType.MESH))
    pl.semaphore_wait(barrier, n - 1 + groups - 1)

    def send_ids(j):
        shard_copy(IDS, ids_ref, idg.at[mine, me], j, me).start()
        shard_copy(COT, cot_ref, cotg.at[me], j, me).start()

    peers(send_ids)
    idg[mine, me] = ids_ref[...]
    cotg[me] = cot_ref[...]

    spare = jnp.zeros((samples - width, samples), F32)
    hot_col[...] = jnp.concatenate([hot_rows[...].astype(F32), spare], axis=0).T.astype(I32)
    chunk = min(512, table_rows)
    pooled = jnp.zeros((samples, embed), F32)
    lane = lax.broadcasted_iota(I32, (samples, chunk), 1)
    for c in range(table_rows // chunk):
        count = jnp.zeros((samples, chunk), F32)
        for k in range(width):
            count = count + jnp.where(hot_col[:, k : k + 1] - c * chunk == lane, 1.0, 0.0)
        pooled = pooled + dot(count.astype(BF16), hot_table[c * chunk : (c + 1) * chunk, :])
    hot_src[...] = pooled.astype(BF16)
    gather_start(HOTIN, hot_src, hot_view)
    ing[me, :, 0:embed] = hot_src[...]

    lookups = 2 * samples
    row_i = lax.broadcasted_iota(I32, (lookups, lookups), 0)
    col_i = lax.broadcasted_iota(I32, (lookups, lookups), 1)
    tri[...] = jnp.where(row_i < col_i, 1.0, 0.0).astype(BF16)

    def lookup_rows(block, first):
        return jnp.concatenate([block[first : first + 1], block[first + 1 : first + 2]], axis=1)

    own_block = ids_ref[...]
    owner = lookup_rows(own_block, width)
    match = jnp.where(lax.broadcasted_iota(I32, (n, lookups), 0) == owner, 1.0, 0.0)
    order = dot(match.astype(BF16), tri[...])
    place = owner * cap + jnp.sum(match * order, axis=0, keepdims=True).astype(I32)
    slot_i = lax.broadcasted_iota(I32, (slots, lookups), 0)
    first = 2 * lax.broadcasted_iota(I32, (lookups, samples), 1)
    lookup_i = lax.broadcasted_iota(I32, (lookups, samples), 0)
    pair = jnp.where((lookup_i == first) | (lookup_i == first + 1), 1.0, 0.0).astype(BF16)
    pick[...] = dot(jnp.where(slot_i == place, 1.0, 0.0).astype(BF16), pair).astype(BF16)

    cap_i = lax.broadcasted_iota(I32, (cap, lookups), 0)

    def find(d):
        hits = [jnp.where(lookup_rows(idg[d, j], width) == me, 1.0, 0.0) for j in range(n)]
        positions = dot(jnp.concatenate(hits, axis=0).astype(BF16), tri[...]).astype(I32)
        for j in range(n):
            chosen = jnp.where(cap_i == positions[j : j + 1], hits[j], 0.0).astype(BF16)
            offset = lookup_rows(idg[d, j], width + 2)
            high = jnp.broadcast_to((offset >> 6).astype(F32), (embed, lookups)).astype(BF16)
            low = jnp.broadcast_to((offset & 63).astype(F32), (embed, lookups)).astype(BF16)
            offc[j * cap : (j + 1) * cap, :] = dot_nt(chosen, high) * 64.0 + dot_nt(chosen, low)

    tall = 64

    def turn(place_at):
        row = offc[...].T[0:1].astype(I32)
        down = lax.broadcasted_iota(I32, (tall, slots), 0)
        for c in range(owned // tall):
            turned[place_at, c * tall : (c + 1) * tall, :] = jnp.where(
                row - c * tall == down, 1.0, 0.0
            ).astype(BF16)

    peers(lambda j: shard_copy(IDS, ids_ref, idg.at[mine, j], j, j).wait_recv())
    dp_peers(lambda d: dp_copy(DIDS, idg.at[mine], idg.at[mine], d, mine).start())
    find(mine)
    across = lax.broadcasted_iota(I32, (slots, embed), 1)
    offsets = offc[...].astype(I32)
    for c in range(owned // embed):
        onehot[:, c * embed : (c + 1) * embed] = jnp.where(
            offsets - c * embed == across, 1.0, 0.0
        ).astype(BF16)
    rows_src[...] = dot(onehot[...], cold_table[...]).astype(BF16).reshape(n, cap, embed)
    peers(lambda j: shard_copy(ROWS, rows_src.at[j], answer.at[me], j, me).start())
    answer[me] = rows_src[me]
    gather_pass(HOTIN, hot_src, hot_view)

    if keep_all:
        turn(mine)

    kept_i = lax.broadcasted_iota(I32, (kept, samples), 0) + me * kept
    for j in range(n):
        count = jnp.zeros((kept, samples), F32)
        for k in range(width):
            count = count + jnp.where(idg[mine, j, k : k + 1, :] == kept_i, 1.0, 0.0)
        hot_counts[:, j * samples : (j + 1) * samples] = count.astype(BF16)

    peers(lambda j: shard_copy(ROWS, rows_src.at[j], answer.at[j], j, j).wait_recv())
    cold_src[...] = dot_tn(pick[...], answer[...].reshape(slots, embed)).astype(BF16)
    gather_start(COLDIN, cold_src, cold_view)
    ing[me, :, embed : 2 * embed] = cold_src[...]

    def other_tables(low, high):
        def step(i, carry):
            d = lax.rem(mine + groups - i, groups)
            dp_copy(DIDS, idg.at[mine], idg.at[d], d, d).wait_recv()
            if keep_all:
                find(d)
                turn(d)
            return carry

        lax.fori_loop(low, high, step, 0)

    half = 1 + groups // 2
    other_tables(1, 2)
    gather_pass(COLDIN, cold_src, cold_view)
    other_tables(2, half)

    head_rows = jnp.broadcast_to(w_out[...], (16, hidden_dev))

    def dense(i, carry):
        j = lax.rem(me + i, n)

        @pl.when(lax.rem(i, 2) == 1)
        def _():
            shard_copy(HOTIN, hot_src, ing.at[j, :, pl.ds(0, embed)], j, j).wait_recv()
            shard_copy(COLDIN, cold_src, ing.at[j, :, pl.ds(embed, embed)], j, j).wait_recv()

        @pl.when(i > 0)
        def _():
            shard_copy(COT, cot_ref, cotg.at[j], j, j).wait_recv()

        pre = dot(ing[j], w_in[...]) + bias[...].astype(F32)
        sigma = jax.nn.sigmoid(pre)
        hidden = (pre * sigma).astype(BF16)
        logit_src[j] = dot_nt(head_rows, hidden)[0:8]
        cot = jnp.broadcast_to(cotg[j][0:1], (samples, samples)).T
        cot = jnp.concatenate([cot] * (hidden_dev // samples), axis=1)
        slope = sigma * (1.0 + pre * (1.0 - sigma))
        grad = (cot * w_out[...].astype(F32) * slope).astype(BF16)
        grads[j] = grad
        part_src[j] = dot_nt(grad, w_in[...]).astype(BF16)

        @pl.when(i > 0)
        def _():
            shard_copy(PART, part_src.at[j], part_in.at[me], j, me).start()
            shard_copy(LOGIT, logit_src.at[j], logit_in.at[me], j, me).start()

        return carry

    lax.fori_loop(0, n, dense, 0)
    part_in[me] = part_src[me]
    logit_in[me] = logit_src[me]

    weight_in[mine] = dot_tn(
        ing[...].reshape(group, 2 * embed), grads[...].reshape(group, hidden_dev)
    ).astype(BF16)
    dp_peers(lambda d: dp_copy(DWEIGHT, weight_in.at[mine], weight_in.at[mine], d, mine).start())

    other_tables(half, groups)

    def add_part(i, total):
        j = lax.rem(me + i, n)

        @pl.when(i > 0)
        def _():
            shard_copy(PART, part_src.at[j], part_in.at[j], j, j).wait_recv()

        return total + part_in[j].astype(F32)

    total = lax.fori_loop(0, n, add_part, jnp.zeros((samples, 2 * embed), F32))
    total = total.astype(BF16)
    hotg_src[...] = total[:, 0:embed]
    slot_src[...] = dot(pick[...], total[:, embed:]).astype(BF16).reshape(n, cap, embed)

    def send_grads(j):
        shard_copy(COLDG, slot_src.at[j], slot_in.at[mine, me], j, me).start()

    peers(send_grads)
    gather_start(HOTG, hotg_src, grad_view)
    slot_in[mine, me] = slot_src[me]
    hotg_in[me] = hotg_src[...]
    gather_pass(HOTG, hotg_src, grad_view)

    peers(lambda j: shard_copy(COLDG, slot_src.at[j], slot_in.at[mine, j], j, j).wait_recv())
    dp_peers(lambda d: dp_copy(DCOLD, slot_in.at[mine], slot_in.at[mine], d, mine).start())
    shard_copy(HOTG, hotg_src, hotg_in.at[sibling], sibling, sibling).wait_recv()

    def handed(j):
        other = j + 1 - 2 * lax.rem(j, 2)
        shard_copy(HOTG, hotg_src, hotg_in.at[other], other, other).wait_recv()

    same_core(handed)
    hot_in[mine] = dot(hot_counts[...], hotg_in[...].reshape(group, embed)).astype(BF16)
    dp_peers(lambda d: dp_copy(DHOT, hot_in.at[mine], hot_in.at[mine], d, mine).start())

    def add_cold(d):
        where = d
        if not keep_all:
            find(d)
            turn(0)
            where = 0
        gacc[...] += dot(turned[where], slot_in[d].reshape(slots, embed))

    gacc[...] = jnp.zeros_like(gacc)
    add_cold(mine)

    logits = jnp.zeros((8, samples), F32)

    def add_logit(i, total):
        j = lax.rem(me + i, n)

        @pl.when(i > 0)
        def _():
            shard_copy(LOGIT, logit_src.at[j], logit_in.at[j], j, j).wait_recv()

        return total + logit_in[j]

    logit_out[...] = lax.fori_loop(0, n, add_logit, logits)[0:1]

    weight_out[...] = weight_in[mine].astype(F32)

    def add_weight(d):
        dp_copy(DWEIGHT, weight_in.at[mine], weight_in.at[d], d, d).wait_recv()
        weight_out[...] += weight_in[d].astype(F32)

    dp_peers(add_weight)

    def cold_from(d):
        dp_copy(DCOLD, slot_in.at[mine], slot_in.at[d], d, d).wait_recv()
        add_cold(d)

    dp_peers(cold_from)
    cold_out[...] = gacc[...].astype(BF16)

    def hot_from(i, total):
        d = lax.rem(mine + i, groups)

        @pl.when(i > 0)
        def _():
            dp_copy(DHOT, hot_in.at[mine], hot_in.at[d], d, d).wait_recv()

        return total + hot_in[d].astype(F32)

    hot_out[...] = lax.fori_loop(0, groups, hot_from, jnp.zeros((kept, embed), F32)).astype(BF16)

    def sent(j):
        shard_copy(IDS, ids_ref, idg.at[mine, me], j, me).wait_send()
        shard_copy(COT, cot_ref, cotg.at[me], j, me).wait_send()
        shard_copy(HOTIN, hot_src, ing.at[me, :, pl.ds(0, embed)], j, me).wait_send()
        shard_copy(ROWS, rows_src.at[j], answer.at[me], j, me).wait_send()
        shard_copy(COLDIN, cold_src, ing.at[me, :, pl.ds(embed, embed)], j, me).wait_send()
        shard_copy(PART, part_src.at[j], part_in.at[me], j, me).wait_send()
        shard_copy(LOGIT, logit_src.at[j], logit_in.at[me], j, me).wait_send()
        shard_copy(COLDG, slot_src.at[j], slot_in.at[mine, me], j, me).wait_send()
        shard_copy(HOTG, hotg_src, hotg_in.at[me], j, me).wait_send()

    peers(sent)

    def dp_sent(d):
        dp_copy(DIDS, idg.at[mine], idg.at[mine], d, mine).wait_send()
        dp_copy(DWEIGHT, weight_in.at[mine], weight_in.at[mine], d, mine).wait_send()
        dp_copy(DCOLD, slot_in.at[mine], slot_in.at[mine], d, mine).wait_send()
        dp_copy(DHOT, hot_in.at[mine], hot_in.at[mine], d, mine).wait_send()

    dp_peers(dp_sent)


def shards(
    hot_ids, cold_owner, cold_offset, hot_table, cold_table, w_in, bias_in, w_out, cotangent
):
    n = lax.axis_size("shard")
    groups = lax.axis_size("dp")
    samples = hot_ids.shape[0]
    table_rows, embed = hot_table.shape
    owned = cold_table.shape[0]
    inputs_dim, hidden_dev = w_in.shape
    lookups = cold_offset.shape[0]
    cap = max(16, 2 * lookups // n)
    kept = table_rows // n
    slots = n * cap
    keep_all = groups * slots * owned * 2 <= 20 * 2**20
    vmem = pl.BlockSpec(memory_space=pltpu.VMEM)
    logits, hot, cold, weight = pl.pallas_call(
        functools.partial(kernel, n, groups, cap, keep_all),
        out_shape=(
            jax.ShapeDtypeStruct((1, samples), F32),
            jax.ShapeDtypeStruct((kept, embed), BF16),
            jax.ShapeDtypeStruct((owned, embed), BF16),
            jax.ShapeDtypeStruct((inputs_dim, hidden_dev), F32),
        ),
        in_specs=[vmem] * 9,
        out_specs=(vmem,) * 4,
        scratch_shapes=[
            pltpu.VMEM((16, samples), I32),
            pltpu.VMEM((8, samples), F32),
            pltpu.VMEM((samples, samples), I32),
            pltpu.VMEM((groups, n, 16, samples), I32),
            pltpu.VMEM((n, 8, samples), F32),
            pltpu.VMEM((n, samples, 2 * embed), BF16),
            pltpu.VMEM((samples, embed), BF16),
            pltpu.VMEM((samples, embed), BF16),
            pltpu.VMEM((slots, samples), BF16),
            pltpu.VMEM((lookups, lookups), BF16),
            pltpu.VMEM((slots, embed), F32),
            pltpu.VMEM((slots, owned), BF16),
            pltpu.VMEM((groups if keep_all else 1, owned, slots), BF16),
            pltpu.VMEM((n, cap, embed), BF16),
            pltpu.VMEM((n, cap, embed), BF16),
            pltpu.VMEM((kept, n * samples), BF16),
            pltpu.VMEM((n, samples, hidden_dev), BF16),
            pltpu.VMEM((n, samples, 2 * embed), BF16),
            pltpu.VMEM((n, samples, 2 * embed), BF16),
            pltpu.VMEM((n, 8, samples), F32),
            pltpu.VMEM((n, 8, samples), F32),
            pltpu.VMEM((n, cap, embed), BF16),
            pltpu.VMEM((groups, n, cap, embed), BF16),
            pltpu.VMEM((samples, embed), BF16),
            pltpu.VMEM((n, samples, embed), BF16),
            pltpu.VMEM((groups, inputs_dim, hidden_dev), BF16),
            pltpu.VMEM((groups, kept, embed), BF16),
            pltpu.VMEM((owned, embed), F32),
            pltpu.SemaphoreType.DMA((9, n)),
            pltpu.SemaphoreType.DMA((9, n)),
            pltpu.SemaphoreType.DMA((4, groups)),
            pltpu.SemaphoreType.DMA((4, groups)),
        ],
        compiler_params=pltpu.CompilerParams(
            collective_id=0, has_side_effects=True, vmem_limit_bytes=56 * 2**20
        ),
    )(
        hot_ids.T, cold_owner.reshape(2, samples), cold_offset.reshape(2, samples),
        cotangent.reshape(1, samples), hot_table, cold_table, w_in, bias_in, w_out,
    )
    return (logits.reshape(samples), hot, cold, weight)


def solution(mesh):
    in_specs = (
        P(("dp", "shard"), None),
        P(("dp", "shard"), None),
        P(("dp", "shard")),
        P(),
        P("shard", None),
        P(None, "shard"),
        P(None, "shard"),
        P(None, "shard"),
        P(("dp", "shard")),
    )
    out_specs = (P(("dp", "shard")), P("shard", None), P("shard", None), P(None, "shard"))
    return jax.shard_map(shards, mesh=mesh, in_specs=in_specs, out_specs=out_specs, check_vma=False)
```
